32 devices in a mesh: contacts: 8 (over z, y), tm: 4 (over x, core).
Axes of the slice: x: 2, y: 2, z: 4, core: 2. Of those that a mesh axis runs over, the one named last changes fastest.
Arguments:
- signal: bfloat16 [2048, 512], P('contacts', 'tm'), may hold values from -6 to 6
- pos_idx: int32 [2048], P('contacts'), may hold values from 0 to 4095
- live_count: int32 [8], P('contacts'), may hold values from 128 to 256, as said below
- latents: bfloat16 [256, 512], replicated, may hold values from -400 to 400
- pos_table: bfloat16 [4096, 512], replicated, may hold values from -6 to 6
- w_in: bfloat16 [32, 512], replicated, may hold values from -1 to 1
- w_kv: bfloat16 [512, 1024], replicated, may hold values from -0.25 to 0.25
- w_query: bfloat16 [512, 512], replicated, may hold values from -0.25 to 0.25
- w_out: bfloat16 [512, 512], replicated, may hold values from -0.25 to 0.25
- conv_weight: bfloat16 [2, 3, 512, 512], replicated, may hold values from -0.15625 to 0.15625
- conv_bias: float32 [2, 512], replicated, may hold values from -3 to 3
- cotangent: bfloat16 [16, 256, 512], P('tm', 'contacts'), may hold values from -6 to 6
Outputs:
- features: bfloat16 [16, 256, 512], P('tm', 'contacts')
- d_latents: float32 [256, 512], replicated
The draws below stay inside these ranges and needn't reach their ends.
Inputs may be any that keep to these rules, and one draw needn't show every extreme that they name: The first live_count[b] contacts of block b are valid; some block is full and some block has exactly 128 valid contacts.
All inputs are finite; a program needn't handle non-finite values.
Results may differ from the reference program's by a relative error of at most 0.018.
The reference program's roundings to bfloat16 on the way count: a program that leaves them out, or rounds other values in their place, can miss the bound.
Values may be sent and summed in bfloat16 or wider, within the bound.
A program may use at most 192 MiB of HBM per device.

```python
import jax
import jax.numpy as jnp
from jax import lax

D = 512
HD = 64
LAT = 256
POS = 4096
PATCH = 32
KSIZE = 3
LAYERS = 2
CON_DEV = 256
CONTACTS = 2048
NPATCH = 16
SAMPLES = 512
N_CONTACTS = 8


def draw_latents(key, part):
    key_base = jax.random.fold_in(key, 0)
    base_vals = jax.random.normal(key_base, (LAT, D), jnp.float32)
    base_vals = jnp.clip(base_vals, -4.0, 4.0)
    return base_vals.astype(jnp.bfloat16)


def draw_live_count(key, part):
    key_vals = jax.random.fold_in(key, 701)
    key_order = jax.random.fold_in(key, 702)
    counts = jax.random.randint(key_vals, (N_CONTACTS,), CON_DEV // 2, CON_DEV + 1, dtype=jnp.int32)
    order = jax.random.permutation(key_order, N_CONTACTS)
    slots = jnp.arange(N_CONTACTS, dtype=jnp.int32)
    counts = jnp.where(slots == order[0], CON_DEV, counts)
    counts = jnp.where(slots == order[1], CON_DEV // 2, counts)
    return counts.astype(jnp.int32)


def touch_ends(entries, stream_key, least, top_value):
    spot = [jax.random.randint(jax.random.fold_in(stream_key, axis), (), 0, length) for axis, length in enumerate(entries.shape)]
    main_axis = entries.shape.index(max(entries.shape))
    next_to = spot[:main_axis] + [(spot[main_axis] + 1) % entries.shape[main_axis]] + spot[main_axis + 1:]
    return entries.at[tuple(spot)].set(least).at[tuple(next_to)].set(top_value)


def block_scale(rng, extent, cuts, low, top_value):
    gain, own = 1.0, jax.random.fold_in(rng, 6)
    for dim, shards_of in cuts:
        draws = jnp.exp(jax.random.uniform(jax.random.fold_in(own, dim), (shards_of,), jnp.float32, low / len(cuts), top_value / len(cuts)))
        gain = gain * jnp.repeat(draws, extent[dim] // shards_of).reshape([-1 if axis == dim else 1 for axis in range(len(extent))])
    return gain


def gaussian(rng, extent, scale, most, shards=(), kind=jnp.bfloat16):
    array = jax.random.normal(rng, extent, jnp.float32) * scale
    if len(shards) > 0:
        array = block_scale(rng, extent, shards, -0.22, 0.18) * array
    return jnp.clip(array, min=-most, max=most).astype(kind)


def setup_inputs(seed: int = 0) -> dict:
    streams_of = jax.random.split(jax.random.key(seed), 13)
    return {
        "signal": gaussian(streams_of[0], (CONTACTS, SAMPLES), 1.0, 6.0, ((0, 8), (1, 4))),
        "pos_idx": touch_ends(jax.random.randint(streams_of[1], (CONTACTS,), 0, POS), jax.random.fold_in(streams_of[1], 1), 0, POS - 1).astype(jnp.int32),
        "live_count": draw_live_count(jax.random.fold_in(streams_of[12], 71), 0),
        "latents": draw_latents(jax.random.fold_in(streams_of[12], 71), 0),
        "pos_table": gaussian(streams_of[4], (POS, D), 1.0, 6.0),
        "w_in": gaussian(streams_of[5], (PATCH, D), PATCH ** -0.5, 1.0),
        "w_kv": gaussian(streams_of[6], (D, 2 * D), D ** -0.5, 0.25),
        "w_query": gaussian(streams_of[7], (D, D), D ** -0.5, 0.25),
        "w_out": gaussian(streams_of[8], (D, D), D ** -0.5, 0.25),
        "conv_weight": gaussian(streams_of[9], (LAYERS, KSIZE, D, D), (3 * D) ** -0.5, 0.15625),
        "conv_bias": gaussian(streams_of[10], (LAYERS, D), 0.5, 3.0, (), jnp.float32),
        "cotangent": gaussian(streams_of[11], (NPATCH, LAT, D), 1.0, 6.0, ((0, 4), (1, 8))),
    }


neg_big = -1.0e30
scale_dot = 0.125


def rounded(value):
    return lax.optimization_barrier(value.astype(jnp.bfloat16))


def silu_slope(pre_act):
    sigmoid_v = jax.nn.sigmoid(pre_act)
    return sigmoid_v * (1.0 + pre_act * (1.0 - sigmoid_v))


def reference(signal, pos_idx, live_count, latents, pos_table, w_in, w_kv, w_query, w_out, conv_weight, conv_bias, cotangent):
    head_count = D // HD
    contact_ids = jnp.arange(CONTACTS, dtype=jnp.int32)
    is_valid = (contact_ids % CON_DEV) < jnp.repeat(live_count, CON_DEV)
    pos_rows = jnp.take(pos_table, pos_idx, axis=0).astype(jnp.float32)
    queries = rounded(jnp.dot(latents, w_query, preferred_element_type=jnp.float32))
    query_f = queries.astype(jnp.float32).reshape(LAT, head_count, HD)

    def patch_keys(patch_idx):
        sig_piece = lax.dynamic_slice_in_dim(signal, patch_idx * PATCH, PATCH, 1)
        embedded = jnp.dot(sig_piece, w_in, preferred_element_type=jnp.float32)
        tokens = rounded(embedded + pos_rows)
        keyval = rounded(jnp.dot(tokens, w_kv, preferred_element_type=jnp.float32)).astype(jnp.float32)
        key_part = keyval[:, :D].reshape(CONTACTS, head_count, HD)
        value_part = keyval[:, D:].reshape(CONTACTS, head_count, HD)
        return key_part, value_part

    def masked_scores(key_part):
        scores = jnp.einsum("ihe,che->hic", query_f, key_part) * scale_dot
        return jnp.where(is_valid, scores, neg_big)

    def forward_patch(patch_idx):
        key_part, value_part = patch_keys(patch_idx)
        scores = masked_scores(key_part)
        top_score = jnp.max(scores, axis=2)
        weights = jnp.where(is_valid, jnp.exp(scores - top_score[..., None]), 0.0)
        totals = jnp.sum(weights, axis=2)
        weights_b = rounded(weights).astype(jnp.float32)
        mixed = jnp.einsum("hic,che->ihe", weights_b, value_part)
        attended = (mixed / jnp.transpose(totals)[:, :, None]).reshape(LAT, D).astype(jnp.bfloat16)
        return attended, top_score, totals

    patch_ids = jnp.arange(NPATCH, dtype=jnp.int32)
    attended, top_all, total_all = lax.map(forward_patch, patch_ids)
    attended = lax.optimization_barrier(attended)

    start_x = rounded(jnp.dot(attended.reshape(NPATCH * LAT, D), w_out, preferred_element_type=jnp.float32)).reshape(NPATCH, LAT, D)
    hidden_list = []
    current = start_x
    for layer_no in range(LAYERS):
        dilation = 2 ** layer_no
        padded = jnp.pad(current, ((dilation, dilation), (0, 0), (0, 0)))
        stacked = jnp.stack([padded[j * dilation: j * dilation + NPATCH] for j in range(KSIZE)], axis=2).astype(jnp.float32)
        pre_act = jnp.einsum("tlji,jio->tlo", stacked, conv_weight[layer_no].astype(jnp.float32)) + conv_bias[layer_no]
        current = rounded(current.astype(jnp.float32) + jax.nn.silu(pre_act))
        hidden_list.append(pre_act)
    features = current

    grad_now = cotangent.astype(jnp.float32)
    for layer_no in reversed(range(LAYERS)):
        dilation = 2 ** layer_no
        grad_pre = rounded(grad_now * silu_slope(hidden_list[layer_no]))
        padded = jnp.pad(grad_pre, ((dilation, dilation), (0, 0), (0, 0)))
        stacked = jnp.stack([padded[(KSIZE - 1 - j) * dilation: (KSIZE - 1 - j) * dilation + NPATCH] for j in range(KSIZE)], axis=2).astype(jnp.float32)
        grad_now = grad_now + jnp.einsum("tljo,jio->tli", stacked, conv_weight[layer_no].astype(jnp.float32))

    grad_att = rounded(lax.dot_general(rounded(grad_now).reshape(NPATCH * LAT, D), w_out, (((1,), (1,)), ((), ())), preferred_element_type=jnp.float32)).reshape(NPATCH, LAT, D)
    delta_row = jnp.sum(grad_att.astype(jnp.float32).reshape(NPATCH, LAT, head_count, HD) * attended.astype(jnp.float32).reshape(NPATCH, LAT, head_count, HD), axis=3)

    def back_patch(dq_sum, patch_idx):
        key_part, value_part = patch_keys(patch_idx)
        scores = masked_scores(key_part)
        top_now = top_all[patch_idx]
        total_now = total_all[patch_idx]
        prob_vals = jnp.where(is_valid, jnp.exp(scores - top_now[..., None]) / total_now[..., None], 0.0)
        grad_rows = grad_att[patch_idx].astype(jnp.float32).reshape(LAT, head_count, HD)
        grad_prob = jnp.einsum("ihe,che->hic", grad_rows, value_part)
        delta_now = jnp.transpose(delta_row[patch_idx])
        dscore = rounded(prob_vals * (grad_prob - delta_now[..., None])).astype(jnp.float32)
        return dq_sum + jnp.einsum("hic,che->ihe", dscore, key_part), None

    dq_sum, unused = lax.scan(back_patch, jnp.zeros((LAT, head_count, HD), jnp.float32), patch_ids)
    query_grad = (dq_sum * scale_dot).reshape(LAT, D)
    d_latents = lax.dot_general(rounded(query_grad), w_query, (((1,), (1,)), ((), ())), preferred_element_type=jnp.float32)
    return features, d_latents
```

```python
import functools

import jax
import jax.numpy as jnp
from jax import lax
from jax.experimental import pallas as pl
from jax.experimental.pallas import tpu as pltpu
from jax.sharding import PartitionSpec as P

HD = 64
PATCH = 32
KSIZE = 3
LAYERS = 2


neg_big = -1e30
scale_dot = 0.125


def with_halo(x, sides, width):
    for axis, dim in sides:
        peers, length = (lax.axis_size(axis), x.shape[dim])
        up = [(i, (i + 1) % peers) for i in range(peers - 1)]
        down = [(j, i) for i, j in up]
        last = lax.slice_in_dim(x, length - width, length, axis=dim)
        first = lax.slice_in_dim(x, 0, width, axis=dim)
        before = lax.ppermute(last, axis, up)
        after = lax.ppermute(first, axis, down)
        x = jnp.concatenate([before, x, after], axis=dim)
    return x


def silu_slope(pre_act):
    sigmoid_v = jax.nn.sigmoid(pre_act)
    return sigmoid_v * (1.0 + pre_act * (1.0 - sigmoid_v))


def split_heads(values, head_count):
    return values.reshape(values.shape[:-1] + (head_count, values.shape[-1] // head_count))


def normalize(accum_out, totals):
    head_count = totals.shape[-1]
    return (
        (split_heads(accum_out, head_count) / totals[..., None])
        .reshape(accum_out.shape)
        .astype(jnp.bfloat16)
    )


def conv_apply(source, weight, bias_row, dilation, out_count):
    stacked = jnp.stack(
        [source[j * dilation : j * dilation + out_count] for j in range(KSIZE)], axis=2
    )
    return (
        jnp.einsum("tlji,jio->tlo", stacked, weight, preferred_element_type=jnp.float32) + bias_row
    )


def local(
    signal,
    pos_idx,
    live_count,
    latents,
    pos_table,
    w_in,
    w_kv,
    w_query,
    w_out,
    conv_weight,
    conv_bias,
    cotangent,
):
    con_dev = signal.shape[0]
    pat_dev = signal.shape[1] // PATCH
    model_width = w_query.shape[0]
    head_count = model_width // HD
    lat_rows = latents.shape[0]
    groups = lax.axis_size("contacts")
    lat_dev = lat_rows // groups
    is_valid = jnp.arange(con_dev, dtype=jnp.int32) < live_count[0]
    embedded = jnp.einsum(
        "cpt,td->pcd",
        signal.reshape(con_dev, pat_dev, PATCH),
        w_in,
        preferred_element_type=jnp.float32,
    )
    pos_rows = jnp.take(pos_table, pos_idx, axis=0).astype(jnp.float32)
    tokens = (embedded + pos_rows[None]).astype(jnp.bfloat16)
    keyval = jnp.dot(
        tokens.reshape(pat_dev * con_dev, model_width), w_kv, preferred_element_type=jnp.float32
    ).astype(jnp.bfloat16)
    keyval = keyval.reshape(pat_dev // 2, 2, con_dev, 2, head_count, HD)
    queries = (
        jnp.dot(latents, w_query, preferred_element_type=jnp.float32)
        .astype(jnp.bfloat16)
        .reshape(lat_rows, head_count, HD)
    )

    def masked_scores(key_block):
        scores = (
            jnp.einsum("ihe,pche->phic", queries, key_block, preferred_element_type=jnp.float32)
            * scale_dot
        )
        return jnp.where(is_valid, scores, neg_big)

    def attend(kv_block):
        scores = masked_scores(kv_block[:, :, 0])
        top_score = jnp.max(scores, axis=3)
        weights = jnp.where(is_valid, jnp.exp(scores - top_score[..., None]), 0.0)
        totals = jnp.sum(weights, axis=3)
        accum_out = jnp.einsum(
            "phic,pche->pihe",
            weights.astype(jnp.bfloat16),
            kv_block[:, :, 1],
            preferred_element_type=jnp.float32,
        )
        return (
            jnp.swapaxes(top_score, 1, 2),
            jnp.swapaxes(totals, 1, 2),
            accum_out.reshape(2, lat_rows, model_width),
        )

    top_score, totals, accum_out = lax.map(attend, keyval)
    top_score = top_score.reshape(pat_dev, lat_rows, head_count)
    totals = totals.reshape(pat_dev, lat_rows, head_count)
    accum_out = accum_out.reshape(pat_dev, lat_rows, model_width)
    got_top, got_total, got_acc = (
        lax.all_to_all(top_score[None], "contacts", split_axis=2, concat_axis=0, tiled=True),
        lax.all_to_all(totals[None], "contacts", split_axis=2, concat_axis=0, tiled=True),
        lax.all_to_all(accum_out[None], "contacts", split_axis=2, concat_axis=0, tiled=True),
    )
    own_top = jnp.max(got_top, axis=0)
    factor = jnp.exp(got_top - own_top[None])
    own_total = jnp.sum(got_total * factor, axis=0)
    own_acc = jnp.sum(split_heads(got_acc, head_count) * factor[..., None], axis=0).reshape(
        pat_dev, lat_dev, model_width
    )
    attended = normalize(own_acc, own_total)
    start_x = (
        jnp.dot(
            attended.reshape(pat_dev * lat_dev, model_width),
            w_out,
            preferred_element_type=jnp.float32,
        )
        .astype(jnp.bfloat16)
        .reshape(pat_dev, lat_dev, model_width)
    )
    hidden_list = []
    current = start_x
    for layer_no in range(LAYERS):
        dilation = 2**layer_no
        padded = with_halo(current, (("tm", 0),), dilation * (KSIZE // 2))
        pre_act = conv_apply(padded, conv_weight[layer_no], conv_bias[layer_no], dilation, pat_dev)
        current = (current.astype(jnp.float32) + jax.nn.silu(pre_act)).astype(jnp.bfloat16)
        hidden_list.append(pre_act)
    grad_now = cotangent.astype(jnp.float32)
    for layer_no in reversed(range(LAYERS)):
        dilation = 2**layer_no
        grad_pre = (grad_now * silu_slope(hidden_list[layer_no])).astype(jnp.bfloat16)
        padded = with_halo(grad_pre, (("tm", 0),), dilation * (KSIZE // 2))
        stacked = jnp.stack(
            [
                padded[(KSIZE - 1 - j) * dilation : (KSIZE - 1 - j) * dilation + pat_dev]
                for j in range(KSIZE)
            ],
            axis=2,
        )
        grad_now = grad_now + jnp.einsum(
            "tljo,jio->tli", stacked, conv_weight[layer_no], preferred_element_type=jnp.float32
        )
    grad_att = lax.dot_general(
        grad_now.astype(jnp.bfloat16).reshape(pat_dev * lat_dev, model_width),
        w_out,
        (((1,), (1,)), ((), ())),
        preferred_element_type=jnp.float32,
    )
    grad_att = grad_att.astype(jnp.bfloat16).reshape(pat_dev, lat_dev, model_width)
    grad_all, attended_all = (
        lax.all_gather(grad_att, "contacts", axis=1, tiled=True),
        lax.all_gather(attended, "contacts", axis=1, tiled=True),
    )
    top_all, total_all = (
        lax.all_gather(own_top, "contacts", axis=1, tiled=True),
        lax.all_gather(own_total, "contacts", axis=1, tiled=True),
    )
    delta_row = jnp.sum(
        split_heads(grad_all.astype(jnp.float32), head_count)
        * split_heads(attended_all.astype(jnp.float32), head_count),
        axis=3,
    )

    def back_block(dq_sum, parts):
        kv_block, grad_block, top_block, total_block, delta_block = parts
        key_block = kv_block[:, :, 0]
        scores = masked_scores(key_block)
        top_now = jnp.swapaxes(top_block, 1, 2)
        total_now = jnp.swapaxes(total_block, 1, 2)
        prob_vals = jnp.where(
            is_valid, jnp.exp(scores - top_now[..., None]) / total_now[..., None], 0.0
        )
        grad_prob = jnp.einsum(
            "pihe,pche->phic",
            split_heads(grad_block, head_count),
            kv_block[:, :, 1],
            preferred_element_type=jnp.float32,
        )
        delta_now = jnp.swapaxes(delta_block, 1, 2)
        dscore = (prob_vals * (grad_prob - delta_now[..., None])).astype(jnp.bfloat16)
        return (
            dq_sum
            + jnp.einsum("phic,pche->ihe", dscore, key_block, preferred_element_type=jnp.float32),
            None,
        )

    pairs = pat_dev // 2
    dq_sum, unused = lax.scan(
        back_block,
        jnp.zeros((lat_rows, head_count, HD), jnp.float32),
        (
            keyval,
            grad_all.reshape(pairs, 2, lat_rows, model_width),
            top_all.reshape(pairs, 2, lat_rows, head_count),
            total_all.reshape(pairs, 2, lat_rows, head_count),
            delta_row.reshape(pairs, 2, lat_rows, head_count),
        ),
    )
    query_grad = lax.psum((dq_sum * scale_dot).reshape(lat_rows, model_width), ("contacts", "tm"))
    d_latents = lax.dot_general(
        query_grad.astype(jnp.bfloat16),
        w_query,
        (((1,), (1,)), ((), ())),
        preferred_element_type=jnp.float32,
    )
    return (current, d_latents)


MESH = pl.DeviceIdType.MESH
HALO = 3
CHUNK = 512
VMEM_CAP = 56 * 1024 * 1024


def dot_nn(lhs, rhs):
    return jnp.dot(lhs, rhs, preferred_element_type=jnp.float32)


def dot_nt(lhs, rhs):
    return lax.dot_general(lhs, rhs, (((1,), (1,)), ((), ())), preferred_element_type=jnp.float32)


def fused_kernel(
    groups,
    times,
    sig_ref,
    idx_ref,
    latents_ref,
    w_in_ref,
    w_query_ref,
    bias_ref,
    cot_ref,
    table_hbm,
    w_kv_hbm,
    w_out_hbm,
    conv_hbm,
    feat_ref,
    dlat_ref,
    table_ref,
    w_kv_ref,
    w_out_ref,
    conv_ref,
    sig_all,
    idx_all,
    w_wide,
    pos_rows,
    valid_ref,
    kv_ref,
    exp_ref,
    prob_ref,
    inv_tot,
    q_wide,
    att_ref,
    cot_halo,
    x_ext,
    g_ext,
    gpre_ref,
    g1_ref,
    dq_acc,
    dq_parts,
    dq_all,
    load_sem,
    idx_send,
    idx_recv,
    sig_send,
    sig_recv,
    halo_send,
    halo_recv,
    part_send,
    part_recv,
    all_send,
    all_recv,
):
    me = lax.axis_index("contacts")
    tm = lax.axis_index("tm")
    con_dev, width_sig = sig_ref.shape
    pat_dev = width_sig // PATCH
    lat_dev, width = att_ref.shape[1:]
    heads = width // HD
    rows = heads * lat_dev
    contacts = groups * con_dev
    table_rows = table_ref.shape[0]

    loads = [
        pltpu.make_async_copy(src, dst, load_sem.at[n])
        for n, (src, dst) in enumerate(
            (
                (table_hbm, table_ref),
                (w_kv_hbm, w_kv_ref),
                (w_out_hbm, w_out_ref),
                (conv_hbm, conv_ref),
            )
        )
    ]
    for load in loads:
        load.start()

    barrier = pltpu.get_barrier_semaphore()
    for k in range(1, groups):
        pl.semaphore_signal(
            barrier, inc=1, device_id=(lax.rem(me + k, groups), tm), device_id_type=MESH
        )
    for k in range(1, times):
        pl.semaphore_signal(
            barrier, inc=1, device_id=(me, lax.rem(tm + k, times)), device_id_type=MESH
        )
    pl.semaphore_wait(barrier, groups + times - 2)

    def remote(src, dst, send, recv, contact_id, tm_id):
        return pltpu.make_async_remote_copy(
            src_ref=src,
            dst_ref=dst,
            send_sem=send,
            recv_sem=recv,
            device_id=(contact_id, tm_id),
            device_id_type=MESH,
        )

    def idx_copy(k):
        return remote(
            idx_ref, idx_all.at[me], idx_send.at[k], idx_recv.at[k], lax.rem(me + k, groups), tm
        )

    def sig_copy(k):
        return remote(
            sig_ref, sig_all.at[me], sig_send.at[k], sig_recv.at[k], lax.rem(me + k, groups), tm
        )

    def to_right(src, dst, n):
        return remote(src, dst, halo_send.at[n], halo_recv.at[n], me, tm + 1)

    def to_left(src, dst, n):
        return remote(src, dst, halo_send.at[n], halo_recv.at[n], me, tm - 1)

    has_left = tm > 0
    has_right = tm < times - 1

    cot_pair = (
        to_right(cot_ref.at[pl.ds(pat_dev - 1, 1)], cot_halo.at[pl.ds(0, 1)], 0),
        to_left(cot_ref.at[pl.ds(0, 1)], cot_halo.at[pl.ds(1, 1)], 1),
    )

    def ext_pair(ext, n):
        return (
            to_right(ext.at[pl.ds(pat_dev, HALO)], ext.at[pl.ds(0, HALO)], n),
            to_left(ext.at[pl.ds(HALO, HALO)], ext.at[pl.ds(HALO + pat_dev, HALO)], n + 1),
        )

    x_pair = ext_pair(x_ext, 2)
    g_pair = ext_pair(g_ext, 4)

    def start_pair(pair):
        @pl.when(has_right)
        def _():
            pair[0].start()

        @pl.when(has_left)
        def _():
            pair[1].start()

    def arrive_pair(pair):
        @pl.when(has_left)
        def _():
            pair[0].wait_recv()

        @pl.when(has_right)
        def _():
            pair[1].wait_recv()

    def sent_pair(pair):
        @pl.when(has_right)
        def _():
            pair[0].wait_send()

        @pl.when(has_left)
        def _():
            pair[1].wait_send()

    for k in range(1, groups):
        idx_copy(k).start()
    for k in range(1, groups):
        sig_copy(k).start()
    start_pair(cot_pair)

    @pl.when(jnp.logical_not(has_left))
    def _():
        x_ext[0:HALO] = jnp.zeros((HALO, lat_dev, width), jnp.bfloat16)
        g_ext[0:HALO] = jnp.zeros((HALO, lat_dev, width), jnp.bfloat16)
        cot_halo[0:1] = jnp.zeros((1, lat_dev, width), jnp.bfloat16)

    @pl.when(jnp.logical_not(has_right))
    def _():
        x_ext[HALO + pat_dev :] = jnp.zeros((HALO, lat_dev, width), jnp.bfloat16)
        g_ext[HALO + pat_dev :] = jnp.zeros((HALO, lat_dev, width), jnp.bfloat16)
        cot_halo[1:2] = jnp.zeros((1, lat_dev, width), jnp.bfloat16)

    idx_all[me] = idx_ref[...]
    sig_all[me] = sig_ref[...]

    for p in range(pat_dev):
        w_wide[p] = jnp.zeros((width_sig, width), jnp.bfloat16)
        w_wide[p, p * PATCH : (p + 1) * PATCH, :] = w_in_ref[...]

    own_head = (
        lax.broadcasted_iota(jnp.int32, (rows, width), 0) // lat_dev
        == lax.broadcasted_iota(jnp.int32, (rows, width), 1) // HD
    )

    def widen(values):
        return jnp.where(own_head, jnp.concatenate([values] * heads, axis=0), 0.0)

    def narrow(values):
        return jnp.sum(jnp.where(own_head, values, 0.0).reshape(heads, lat_dev, width), axis=0)

    own_latents = latents_ref[pl.ds(pl.multiple_of(me * lat_dev, lat_dev), lat_dev), :]
    queries = dot_nn(own_latents, w_query_ref[...]).astype(jnp.bfloat16).astype(jnp.float32)
    q_wide[...] = widen(queries * scale_dot).astype(jnp.bfloat16)

    loads[0].wait()

    def gather_block(k, carry):
        @pl.when(k > 0)
        def _():
            idx_copy(k).wait_recv()

        block = lax.rem(me - k + groups, groups)
        idx_rows = idx_all[block]
        start = pl.multiple_of(block * con_dev, con_dev)
        valid_ref[:, pl.ds(start, con_dev)] = jnp.where(idx_rows >= 0, 1.0, 0.0)
        column = jnp.transpose(
            jnp.broadcast_to(idx_rows[0:1].astype(jnp.float32), (128, con_dev))
        ).astype(jnp.int32)[:, 0:1]
        total = jnp.zeros((con_dev, width), jnp.float32)
        for first in range(0, table_rows, CHUNK):
            spots = lax.broadcasted_iota(jnp.int32, (con_dev, CHUNK), 1) + first
            hot = jnp.where(column == spots, 1.0, 0.0).astype(jnp.bfloat16)
            total += dot_nn(hot, table_ref[first : first + CHUNK, :])
        pos_rows[block] = total.astype(jnp.bfloat16)
        return carry

    lax.fori_loop(0, groups, gather_block, 0)
    loads[1].wait()

    def project_block(k, carry):
        @pl.when(k > 0)
        def _():
            sig_copy(k).wait_recv()

        block = lax.rem(me - k + groups, groups)
        sig_block = sig_all[block]
        pos_block = pos_rows[block].astype(jnp.float32)
        start = pl.multiple_of(block * con_dev, con_dev)
        for p in range(pat_dev):
            tokens = (dot_nn(sig_block, w_wide[p]) + pos_block).astype(jnp.bfloat16)
            kv_ref[p, pl.ds(start, con_dev), :] = dot_nn(tokens, w_kv_ref[...]).astype(
                jnp.bfloat16
            )
        return carry

    lax.fori_loop(0, groups, project_block, 0)

    def forward(p, carry):
        top = jnp.full((rows, 1), neg_big, jnp.float32)
        for first in range(0, contacts, CHUNK):
            scores = dot_nt(q_wide[...], kv_ref[p, first : first + CHUNK, 0:width])
            scores = jnp.where(valid_ref[0:1, first : first + CHUNK] > 0.0, scores, neg_big)
            exp_ref[p, :, first : first + CHUNK] = scores
            top = jnp.maximum(top, jnp.max(scores, axis=1, keepdims=True))
        totals = jnp.zeros((rows, 1), jnp.float32)
        for first in range(0, contacts, CHUNK):
            weights = jnp.where(
                valid_ref[0:1, first : first + CHUNK] > 0.0,
                jnp.exp(exp_ref[p, :, first : first + CHUNK] - top),
                0.0,
            )
            exp_ref[p, :, first : first + CHUNK] = weights
            prob_ref[:, first : first + CHUNK] = weights.astype(jnp.bfloat16)
            totals += jnp.sum(weights, axis=1, keepdims=True)
        mixed = dot_nn(prob_ref[...], kv_ref[p, :, width : 2 * width])
        inv_tot[p] = jnp.broadcast_to(1.0 / totals, (rows, 128))
        att_ref[p] = narrow(mixed / totals).astype(jnp.bfloat16)
        return carry

    lax.fori_loop(0, pat_dev, forward, 0)
    loads[2].wait()
    loads[3].wait()

    def flat(values):
        return values.reshape(values.shape[0] * lat_dev, width)

    x_own = dot_nn(flat(att_ref[...]), w_out_ref[...]).astype(jnp.bfloat16)
    x_ext[HALO : HALO + pat_dev] = x_own.reshape(pat_dev, lat_dev, width)
    start_pair(x_pair)
    arrive_pair(x_pair)
    arrive_pair(cot_pair)

    def inside(count, before):
        window = (
            lax.broadcasted_iota(jnp.int32, (count * lat_dev, width), 0) // lat_dev
            + tm * pat_dev
            - before
        )
        return jnp.logical_and(window >= 0, window < times * pat_dev)

    wide0 = pat_dev + 4
    pre0 = bias_ref[0:1, :]
    for j in range(KSIZE):
        pre0 = pre0 + dot_nn(flat(x_ext[j : j + wide0]), conv_ref[0, j])
    x1 = flat(x_ext[1 : 1 + wide0]).astype(jnp.float32) + pre0 * jax.nn.sigmoid(pre0)
    x1 = jnp.where(inside(wide0, 2), x1, 0.0).astype(jnp.bfloat16)
    pre1 = bias_ref[1:2, :]
    span = pat_dev * lat_dev
    for j in range(KSIZE):
        first = 2 * j * lat_dev
        pre1 = pre1 + dot_nn(x1[first : first + span], conv_ref[1, j])
    first = 2 * lat_dev
    x2 = x1[first : first + span].astype(jnp.float32) + pre1 * jax.nn.sigmoid(pre1)
    feat_ref[...] = x2.astype(jnp.bfloat16).reshape(pat_dev, lat_dev, width)

    cot_own = flat(cot_ref[...]).astype(jnp.float32)
    gpre1 = (cot_own * silu_slope(pre1)).astype(jnp.bfloat16)
    g_ext[HALO : HALO + pat_dev] = gpre1.reshape(pat_dev, lat_dev, width)
    start_pair(g_pair)
    arrive_pair(g_pair)

    wide1 = pat_dev + 2
    g1 = jnp.concatenate(
        [cot_halo[0].astype(jnp.float32), cot_own, cot_halo[1].astype(jnp.float32)], axis=0
    )
    for j in range(KSIZE):
        g1 = g1 + dot_nt(flat(g_ext[4 - 2 * j : 4 - 2 * j + wide1]), conv_ref[1, j])
    gpre0 = g1 * silu_slope(pre0[lat_dev : lat_dev + wide1 * lat_dev])
    gpre0 = jnp.where(inside(wide1, 1), gpre0, 0.0).astype(jnp.bfloat16)
    gpre_ref[...] = gpre0.reshape(wide1, lat_dev, width)
    g1_ref[...] = g1
    g0 = dot_nt(flat(gpre_ref[2 : 2 + pat_dev]), conv_ref[0, 0])
    for j in range(1, KSIZE):
        g0 = g0 + dot_nt(flat(gpre_ref[2 - j : 2 - j + pat_dev]), conv_ref[0, j])
    g0 = g0 + g1_ref[lat_dev : lat_dev + span]
    grad_att = dot_nt(g0.astype(jnp.bfloat16), w_out_ref[...]).astype(jnp.bfloat16)
    sent_pair(x_pair)
    x_ext[HALO : HALO + pat_dev] = grad_att.reshape(pat_dev, lat_dev, width)

    dq_acc[...] = jnp.zeros((rows, width), jnp.float32)

    def backward(p, carry):
        grad_wide = widen(x_ext[HALO + p].astype(jnp.float32))
        att_wide = jnp.concatenate([att_ref[p].astype(jnp.float32)] * heads, axis=0)
        delta = jnp.sum(grad_wide * att_wide, axis=1, keepdims=True)
        grad_wide = grad_wide.astype(jnp.bfloat16)
        scale = inv_tot[p][:, 0:1]
        for first in range(0, contacts, CHUNK):
            grad_prob = dot_nt(grad_wide, kv_ref[p, first : first + CHUNK, width : 2 * width])
            prob = exp_ref[p, :, first : first + CHUNK] * scale
            prob_ref[:, first : first + CHUNK] = (prob * (grad_prob - delta)).astype(jnp.bfloat16)
        dq_acc[...] += dot_nn(prob_ref[...], kv_ref[p, :, 0:width])
        return carry

    lax.fori_loop(0, pat_dev, backward, 0)

    dq_parts[tm] = narrow(dq_acc[...]) * scale_dot

    def part_copy(k):
        return remote(
            dq_parts.at[tm],
            dq_parts.at[tm],
            part_send.at[k],
            part_recv.at[k],
            me,
            lax.rem(tm + k, times),
        )

    own_rows = pl.ds(pl.multiple_of(me * lat_dev, lat_dev), lat_dev)

    def all_copy(k):
        return remote(
            dq_all.at[own_rows],
            dq_all.at[own_rows],
            all_send.at[k],
            all_recv.at[k],
            lax.rem(me + k, groups),
            tm,
        )

    for k in range(1, times):
        part_copy(k).start()
    for k in range(1, times):
        part_copy(k).wait_recv()
    dq_sum = dq_parts[0]
    for t in range(1, times):
        dq_sum = dq_sum + dq_parts[t]
    dq_all[own_rows, :] = dq_sum.astype(jnp.bfloat16)
    for k in range(1, groups):
        all_copy(k).start()
    for k in range(1, groups):
        all_copy(k).wait_recv()
    dlat_ref[...] = dot_nt(dq_all[...], w_query_ref[...])

    for k in range(1, groups):
        idx_copy(k).wait_send()
        sig_copy(k).wait_send()
        all_copy(k).wait_send()
    for k in range(1, times):
        part_copy(k).wait_send()
    sent_pair(cot_pair)
    sent_pair(g_pair)


def fused(
    signal,
    pos_idx,
    live_count,
    latents,
    pos_table,
    w_in,
    w_kv,
    w_query,
    w_out,
    conv_weight,
    conv_bias,
    cotangent,
):
    con_dev, width_sig = signal.shape
    pat_dev = width_sig // PATCH
    groups, times = lax.axis_size("contacts"), lax.axis_size("tm")
    lat_rows, width = latents.shape
    lat_dev = lat_rows // groups
    rows = width // HD * lat_dev
    contacts = groups * con_dev
    is_valid = jnp.arange(con_dev, dtype=jnp.int32) < live_count[0]
    spots = jnp.broadcast_to(jnp.where(is_valid, pos_idx, -1)[None], (8, con_dev))
    bf16, f32 = jnp.bfloat16, jnp.float32
    vmem = pl.BlockSpec(memory_space=pltpu.VMEM)
    away = pl.BlockSpec(memory_space=pl.ANY)
    dma = pltpu.SemaphoreType.DMA
    return pl.pallas_call(
        functools.partial(fused_kernel, groups, times),
        out_shape=(
            jax.ShapeDtypeStruct((pat_dev, lat_dev, width), bf16),
            jax.ShapeDtypeStruct((lat_rows, width), f32),
        ),
        in_specs=[vmem] * 7 + [away] * 4,
        out_specs=(vmem, vmem),
        scratch_shapes=[
            pltpu.VMEM(pos_table.shape, bf16),
            pltpu.VMEM(w_kv.shape, bf16),
            pltpu.VMEM(w_out.shape, bf16),
            pltpu.VMEM(conv_weight.shape, bf16),
            pltpu.VMEM((groups, con_dev, width_sig), bf16),
            pltpu.VMEM((groups, 8, con_dev), jnp.int32),
            pltpu.VMEM((pat_dev, width_sig, width), bf16),
            pltpu.VMEM((groups, con_dev, width), bf16),
            pltpu.VMEM((8, contacts), f32),
            pltpu.VMEM((pat_dev, contacts, 2 * width), bf16),
            pltpu.VMEM((pat_dev, rows, contacts), f32),
            pltpu.VMEM((rows, contacts), bf16),
            pltpu.VMEM((pat_dev, rows, 128), f32),
            pltpu.VMEM((rows, width), bf16),
            pltpu.VMEM((pat_dev, lat_dev, width), bf16),
            pltpu.VMEM((2, lat_dev, width), bf16),
            pltpu.VMEM((pat_dev + 2 * HALO, lat_dev, width), bf16),
            pltpu.VMEM((pat_dev + 2 * HALO, lat_dev, width), bf16),
            pltpu.VMEM((pat_dev + 2, lat_dev, width), bf16),
            pltpu.VMEM(((pat_dev + 2) * lat_dev, width), f32),
            pltpu.VMEM((rows, width), f32),
            pltpu.VMEM((times, lat_dev, width), f32),
            pltpu.VMEM((lat_rows, width), bf16),
            dma((4,)),
            dma((groups,)),
            dma((groups,)),
            dma((groups,)),
            dma((groups,)),
            dma((6,)),
            dma((6,)),
            dma((times,)),
            dma((times,)),
            dma((groups,)),
            dma((groups,)),
        ],
        compiler_params=pltpu.CompilerParams(
            collective_id=0, has_side_effects=True, vmem_limit_bytes=VMEM_CAP
        ),
    )(
        signal,
        spots,
        latents,
        w_in,
        w_query,
        conv_bias,
        cotangent,
        pos_table,
        w_kv,
        w_out,
        conv_weight,
    )


def device_program(*args):
    signal, latents = args[0], args[3]
    groups = lax.axis_size("contacts")
    pat_dev = signal.shape[1] // PATCH
    lat_dev = latents.shape[0] // groups
    held = groups * signal.shape[0] * pat_dev * latents.shape[1] * 4
    if lat_dev % 16 == 0 and pat_dev >= HALO and held <= 24 * 1024 * 1024:
        return fused(*args)
    return local(*args)


def solution(mesh):
    in_specs = (
        P("contacts", "tm"),
        P("contacts"),
        P("contacts"),
        P(),
        P(),
        P(),
        P(),
        P(),
        P(),
        P(),
        P(),
        P("tm", "contacts", None),
    )
    out_specs = (P("tm", "contacts", None), P())
    return jax.shard_map(
        device_program, mesh=mesh, in_specs=in_specs, out_specs=out_specs, check_vma=False
    )
```

```python
import functools

import jax
import jax.numpy as jnp
from jax import lax
from jax.experimental import pallas as pl
from jax.experimental.pallas import tpu as pltpu
from jax.sharding import PartitionSpec as P

HD = 64
PATCH = 32
KSIZE = 3
LAYERS = 2


neg_big = -1e30
scale_dot = 0.125


def with_halo(x, sides, width):
    for axis, dim in sides:
        peers, length = (lax.axis_size(axis), x.shape[dim])
        up = [(i, (i + 1) % peers) for i in range(peers - 1)]
        down = [(j, i) for i, j in up]
        last = lax.slice_in_dim(x, length - width, length, axis=dim)
        first = lax.slice_in_dim(x, 0, width, axis=dim)
        before = lax.ppermute(last, axis, up)
        after = lax.ppermute(first, axis, down)
        x = jnp.concatenate([before, x, after], axis=dim)
    return x


def silu_slope(pre_act):
    sigmoid_v = jax.nn.sigmoid(pre_act)
    return sigmoid_v * (1.0 + pre_act * (1.0 - sigmoid_v))


def split_heads(values, head_count):
    return values.reshape(values.shape[:-1] + (head_count, values.shape[-1] // head_count))


def normalize(accum_out, totals):
    head_count = totals.shape[-1]
    return (
        (split_heads(accum_out, head_count) / totals[..., None])
        .reshape(accum_out.shape)
        .astype(jnp.bfloat16)
    )


def conv_apply(source, weight, bias_row, dilation, out_count):
    stacked = jnp.stack(
        [source[j * dilation : j * dilation + out_count] for j in range(KSIZE)], axis=2
    )
    return (
        jnp.einsum("tlji,jio->tlo", stacked, weight, preferred_element_type=jnp.float32) + bias_row
    )


def local(
    signal,
    pos_idx,
    live_count,
    latents,
    pos_table,
    w_in,
    w_kv,
    w_query,
    w_out,
    conv_weight,
    conv_bias,
    cotangent,
):
    con_dev = signal.shape[0]
    pat_dev = signal.shape[1] // PATCH
    model_width = w_query.shape[0]
    head_count = model_width // HD
    lat_rows = latents.shape[0]
    groups = lax.axis_size("contacts")
    lat_dev = lat_rows // groups
    is_valid = jnp.arange(con_dev, dtype=jnp.int32) < live_count[0]
    embedded = jnp.einsum(
        "cpt,td->pcd",
        signal.reshape(con_dev, pat_dev, PATCH),
        w_in,
        preferred_element_type=jnp.float32,
    )
    pos_rows = jnp.take(pos_table, pos_idx, axis=0).astype(jnp.float32)
    tokens = (embedded + pos_rows[None]).astype(jnp.bfloat16)
    keyval = jnp.dot(
        tokens.reshape(pat_dev * con_dev, model_width), w_kv, preferred_element_type=jnp.float32
    ).astype(jnp.bfloat16)
    keyval = keyval.reshape(pat_dev // 2, 2, con_dev, 2, head_count, HD)
    queries = (
        jnp.dot(latents, w_query, preferred_element_type=jnp.float32)
        .astype(jnp.bfloat16)
        .reshape(lat_rows, head_count, HD)
    )

    def masked_scores(key_block):
        scores = (
            jnp.einsum("ihe,pche->phic", queries, key_block, preferred_element_type=jnp.float32)
            * scale_dot
        )
        return jnp.where(is_valid, scores, neg_big)

    def attend(kv_block):
        scores = masked_scores(kv_block[:, :, 0])
        top_score = jnp.max(scores, axis=3)
        weights = jnp.where(is_valid, jnp.exp(scores - top_score[..., None]), 0.0)
        totals = jnp.sum(weights, axis=3)
        accum_out = jnp.einsum(
            "phic,pche->pihe",
            weights.astype(jnp.bfloat16),
            kv_block[:, :, 1],
            preferred_element_type=jnp.float32,
        )
        return (
            jnp.swapaxes(top_score, 1, 2),
            jnp.swapaxes(totals, 1, 2),
            accum_out.reshape(2, lat_rows, model_width),
        )

    top_score, totals, accum_out = lax.map(attend, keyval)
    top_score = top_score.reshape(pat_dev, lat_rows, head_count)
    totals = totals.reshape(pat_dev, lat_rows, head_count)
    accum_out = accum_out.reshape(pat_dev, lat_rows, model_width)
    got_top, got_total, got_acc = (
        lax.all_to_all(top_score[None], "contacts", split_axis=2, concat_axis=0, tiled=True),
        lax.all_to_all(totals[None], "contacts", split_axis=2, concat_axis=0, tiled=True),
        lax.all_to_all(accum_out[None], "contacts", split_axis=2, concat_axis=0, tiled=True),
    )
    own_top = jnp.max(got_top, axis=0)
    factor = jnp.exp(got_top - own_top[None])
    own_total = jnp.sum(got_total * factor, axis=0)
    own_acc = jnp.sum(split_heads(got_acc, head_count) * factor[..., None], axis=0).reshape(
        pat_dev, lat_dev, model_width
    )
    attended = normalize(own_acc, own_total)
    start_x = (
        jnp.dot(
            attended.reshape(pat_dev * lat_dev, model_width),
            w_out,
            preferred_element_type=jnp.float32,
        )
        .astype(jnp.bfloat16)
        .reshape(pat_dev, lat_dev, model_width)
    )
    hidden_list = []
    current = start_x
    for layer_no in range(LAYERS):
        dilation = 2**layer_no
        padded = with_halo(current, (("tm", 0),), dilation * (KSIZE // 2))
        pre_act = conv_apply(padded, conv_weight[layer_no], conv_bias[layer_no], dilation, pat_dev)
        current = (current.astype(jnp.float32) + jax.nn.silu(pre_act)).astype(jnp.bfloat16)
        hidden_list.append(pre_act)
    grad_now = cotangent.astype(jnp.float32)
    for layer_no in reversed(range(LAYERS)):
        dilation = 2**layer_no
        grad_pre = (grad_now * silu_slope(hidden_list[layer_no])).astype(jnp.bfloat16)
        padded = with_halo(grad_pre, (("tm", 0),), dilation * (KSIZE // 2))
        stacked = jnp.stack(
            [
                padded[(KSIZE - 1 - j) * dilation : (KSIZE - 1 - j) * dilation + pat_dev]
                for j in range(KSIZE)
            ],
            axis=2,
        )
        grad_now = grad_now + jnp.einsum(
            "tljo,jio->tli", stacked, conv_weight[layer_no], preferred_element_type=jnp.float32
        )
    grad_att = lax.dot_general(
        grad_now.astype(jnp.bfloat16).reshape(pat_dev * lat_dev, model_width),
        w_out,
        (((1,), (1,)), ((), ())),
        preferred_element_type=jnp.float32,
    )
    grad_att = grad_att.astype(jnp.bfloat16).reshape(pat_dev, lat_dev, model_width)
    grad_all, attended_all = (
        lax.all_gather(grad_att, "contacts", axis=1, tiled=True),
        lax.all_gather(attended, "contacts", axis=1, tiled=True),
    )
    top_all, total_all = (
        lax.all_gather(own_top, "contacts", axis=1, tiled=True),
        lax.all_gather(own_total, "contacts", axis=1, tiled=True),
    )
    delta_row = jnp.sum(
        split_heads(grad_all.astype(jnp.float32), head_count)
        * split_heads(attended_all.astype(jnp.float32), head_count),
        axis=3,
    )

    def back_block(dq_sum, parts):
        kv_block, grad_block, top_block, total_block, delta_block = parts
        key_block = kv_block[:, :, 0]
        scores = masked_scores(key_block)
        top_now = jnp.swapaxes(top_block, 1, 2)
        total_now = jnp.swapaxes(total_block, 1, 2)
        prob_vals = jnp.where(
            is_valid, jnp.exp(scores - top_now[..., None]) / total_now[..., None], 0.0
        )
        grad_prob = jnp.einsum(
            "pihe,pche->phic",
            split_heads(grad_block, head_count),
            kv_block[:, :, 1],
            preferred_element_type=jnp.float32,
        )
        delta_now = jnp.swapaxes(delta_block, 1, 2)
        dscore = (prob_vals * (grad_prob - delta_now[..., None])).astype(jnp.bfloat16)
        return (
            dq_sum
            + jnp.einsum("phic,pche->ihe", dscore, key_block, preferred_element_type=jnp.float32),
            None,
        )

    pairs = pat_dev // 2
    dq_sum, unused = lax.scan(
        back_block,
        jnp.zeros((lat_rows, head_count, HD), jnp.float32),
        (
            keyval,
            grad_all.reshape(pairs, 2, lat_rows, model_width),
            top_all.reshape(pairs, 2, lat_rows, head_count),
            total_all.reshape(pairs, 2, lat_rows, head_count),
            delta_row.reshape(pairs, 2, lat_rows, head_count),
        ),
    )
    query_grad = lax.psum((dq_sum * scale_dot).reshape(lat_rows, model_width), ("contacts", "tm"))
    d_latents = lax.dot_general(
        query_grad.astype(jnp.bfloat16),
        w_query,
        (((1,), (1,)), ((), ())),
        preferred_element_type=jnp.float32,
    )
    return (current, d_latents)


MESH = pl.DeviceIdType.MESH
HALO = 3
CHUNK = 512
VMEM_CAP = 56 * 1024 * 1024


def dot_nn(lhs, rhs):
    return jnp.dot(lhs, rhs, preferred_element_type=jnp.float32)


def dot_nt(lhs, rhs):
    return lax.dot_general(lhs, rhs, (((1,), (1,)), ((), ())), preferred_element_type=jnp.float32)


def fused_kernel(
    groups,
    times,
    sig_ref,
    idx_ref,
    latents_ref,
    w_in_ref,
    w_query_ref,
    bias_ref,
    cot_ref,
    table_hbm,
    w_kv_hbm,
    w_out_hbm,
    conv_hbm,
    feat_ref,
    dlat_ref,
    table_ref,
    w_kv_ref,
    w_out_ref,
    conv_ref,
    sig_all,
    idx_all,
    w_wide,
    pos_rows,
    valid_ref,
    kv_ref,
    exp_ref,
    prob_ref,
    inv_tot,
    q_wide,
    att_ref,
    cot_halo,
    x_ext,
    g_ext,
    gpre_ref,
    g1_ref,
    dq_acc,
    dq_parts,
    dq_all,
    load_sem,
    idx_send,
    idx_recv,
    sig_send,
    sig_recv,
    pos_send,
    pos_recv,
    halo_send,
    halo_recv,
    part_send,
    part_recv,
    all_send,
    all_recv,
):
    me = lax.axis_index("contacts")
    tm = lax.axis_index("tm")
    con_dev, width_sig = sig_ref.shape
    pat_dev = width_sig // PATCH
    lat_dev, width = att_ref.shape[1:]
    heads = width // HD
    rows = heads * lat_dev
    contacts = groups * con_dev
    table_rows = table_ref.shape[0]

    loads = [
        pltpu.make_async_copy(src, dst, load_sem.at[n])
        for n, (src, dst) in enumerate(
            (
                (table_hbm, table_ref),
                (w_kv_hbm, w_kv_ref),
                (w_out_hbm, w_out_ref),
                (conv_hbm, conv_ref),
            )
        )
    ]
    for load in loads:
        load.start()

    barrier = pltpu.get_barrier_semaphore()
    for k in range(1, groups):
        pl.semaphore_signal(
            barrier, inc=1, device_id=(lax.rem(me + k, groups), tm), device_id_type=MESH
        )
    for k in range(1, times):
        pl.semaphore_signal(
            barrier, inc=1, device_id=(me, lax.rem(tm + k, times)), device_id_type=MESH
        )
    pl.semaphore_wait(barrier, groups + times - 2)

    def remote(src, dst, send, recv, contact_id, tm_id):
        return pltpu.make_async_remote_copy(
            src_ref=src,
            dst_ref=dst,
            send_sem=send,
            recv_sem=recv,
            device_id=(contact_id, tm_id),
            device_id_type=MESH,
        )

    def idx_copy(k):
        return remote(
            idx_ref, idx_all.at[me], idx_send.at[k], idx_recv.at[k], lax.rem(me + k, groups), tm
        )

    def sig_copy(k):
        return remote(
            sig_ref, sig_all.at[me], sig_send.at[k], sig_recv.at[k], lax.rem(me + k, groups), tm
        )

    def to_right(src, dst, n):
        return remote(src, dst, halo_send.at[n], halo_recv.at[n], me, tm + 1)

    def to_left(src, dst, n):
        return remote(src, dst, halo_send.at[n], halo_recv.at[n], me, tm - 1)

    has_left = tm > 0
    has_right = tm < times - 1

    cot_pair = (
        to_right(cot_ref.at[pl.ds(pat_dev - 1, 1)], cot_halo.at[pl.ds(0, 1)], 0),
        to_left(cot_ref.at[pl.ds(0, 1)], cot_halo.at[pl.ds(1, 1)], 1),
    )

    def ext_pair(ext, n):
        return (
            to_right(ext.at[pl.ds(pat_dev, HALO)], ext.at[pl.ds(0, HALO)], n),
            to_left(ext.at[pl.ds(HALO, HALO)], ext.at[pl.ds(HALO + pat_dev, HALO)], n + 1),
        )

    x_pair = ext_pair(x_ext, 2)
    g_pair = ext_pair(g_ext, 4)

    def start_pair(pair):
        @pl.when(has_right)
        def _():
            pair[0].start()

        @pl.when(has_left)
        def _():
            pair[1].start()

    def arrive_pair(pair):
        @pl.when(has_left)
        def _():
            pair[0].wait_recv()

        @pl.when(has_right)
        def _():
            pair[1].wait_recv()

    def sent_pair(pair):
        @pl.when(has_right)
        def _():
            pair[0].wait_send()

        @pl.when(has_left)
        def _():
            pair[1].wait_send()

    for k in range(1, groups):
        idx_copy(k).start()
    for k in range(1, groups):
        sig_copy(k).start()
    start_pair(cot_pair)

    @pl.when(jnp.logical_not(has_left))
    def _():
        x_ext[0:HALO] = jnp.zeros((HALO, lat_dev, width), jnp.bfloat16)
        g_ext[0:HALO] = jnp.zeros((HALO, lat_dev, width), jnp.bfloat16)
        cot_halo[0:1] = jnp.zeros((1, lat_dev, width), jnp.bfloat16)

    @pl.when(jnp.logical_not(has_right))
    def _():
        x_ext[HALO + pat_dev :] = jnp.zeros((HALO, lat_dev, width), jnp.bfloat16)
        g_ext[HALO + pat_dev :] = jnp.zeros((HALO, lat_dev, width), jnp.bfloat16)
        cot_halo[1:2] = jnp.zeros((1, lat_dev, width), jnp.bfloat16)

    idx_all[me] = idx_ref[...]
    sig_all[me] = sig_ref[...]

    for p in range(pat_dev):
        w_wide[p] = jnp.zeros((width_sig, width), jnp.bfloat16)
        w_wide[p, p * PATCH : (p + 1) * PATCH, :] = w_in_ref[...]

    own_head = (
        lax.broadcasted_iota(jnp.int32, (rows, width), 0) // lat_dev
        == lax.broadcasted_iota(jnp.int32, (rows, width), 1) // HD
    )

    def widen(values):
        return jnp.where(own_head, jnp.concatenate([values] * heads, axis=0), 0.0)

    def narrow(values):
        return jnp.sum(jnp.where(own_head, values, 0.0).reshape(heads, lat_dev, width), axis=0)

    own_latents = latents_ref[pl.ds(pl.multiple_of(me * lat_dev, lat_dev), lat_dev), :]
    queries = dot_nn(own_latents, w_query_ref[...]).astype(jnp.bfloat16).astype(jnp.float32)
    q_wide[...] = widen(queries * scale_dot).astype(jnp.bfloat16)

    loads[0].wait()

    core = lax.rem(tm, 2)
    sibling = tm + 1 - 2 * core

    def pos_copy(k):
        block = lax.rem(me - k + groups, groups)
        return remote(
            pos_rows.at[block], pos_rows.at[block], pos_send.at[k], pos_recv.at[k], me, sibling
        )

    def mark_valid(k):
        block = lax.rem(me - k + groups, groups)
        start = pl.multiple_of(block * con_dev, con_dev)
        valid_ref[:, pl.ds(start, con_dev)] = jnp.where(idx_all[block] >= 0, 1.0, 0.0)

    def gather_block(pair, carry):
        @pl.when(pair > 0)
        def _():
            idx_copy(2 * pair).wait_recv()

        idx_copy(2 * pair + 1).wait_recv()
        mark_valid(2 * pair)
        mark_valid(2 * pair + 1)
        k = 2 * pair + core
        block = lax.rem(me - k + groups, groups)
        idx_rows = idx_all[block]
        column = jnp.transpose(
            jnp.broadcast_to(idx_rows[0:1].astype(jnp.float32), (128, con_dev))
        ).astype(jnp.int32)[:, 0:1]
        total = jnp.zeros((con_dev, width), jnp.float32)
        for first in range(0, table_rows, CHUNK):
            spots = lax.broadcasted_iota(jnp.int32, (con_dev, CHUNK), 1) + first
            hot = jnp.where(column == spots, 1.0, 0.0).astype(jnp.bfloat16)
            total += dot_nn(hot, table_ref[first : first + CHUNK, :])
        pos_rows[block] = total.astype(jnp.bfloat16)
        pos_copy(k).start()
        return carry

    lax.fori_loop(0, groups // 2, gather_block, 0)
    loads[1].wait()

    def project_block(k, carry):
        @pl.when(k > 0)
        def _():
            sig_copy(k).wait_recv()

        @pl.when(lax.rem(k, 2) != core)
        def _():
            pos_copy(k).wait_recv()

        block = lax.rem(me - k + groups, groups)
        sig_block = sig_all[block]
        pos_block = pos_rows[block].astype(jnp.float32)
        start = pl.multiple_of(block * con_dev, con_dev)
        for p in range(pat_dev):
            tokens = (dot_nn(sig_block, w_wide[p]) + pos_block).astype(jnp.bfloat16)
            kv_ref[p, pl.ds(start, con_dev), :] = dot_nn(tokens, w_kv_ref[...]).astype(
                jnp.bfloat16
            )
        return carry

    lax.fori_loop(0, groups, project_block, 0)

    def forward(p, carry):
        top = jnp.full((rows, 1), neg_big, jnp.float32)
        for first in range(0, contacts, CHUNK):
            scores = dot_nt(q_wide[...], kv_ref[p, first : first + CHUNK, 0:width])
            scores = jnp.where(valid_ref[0:1, first : first + CHUNK] > 0.0, scores, neg_big)
            exp_ref[p, :, first : first + CHUNK] = scores
            top = jnp.maximum(top, jnp.max(scores, axis=1, keepdims=True))
        totals = jnp.zeros((rows, 1), jnp.float32)
        for first in range(0, contacts, CHUNK):
            weights = jnp.exp(exp_ref[p, :, first : first + CHUNK] - top)
            exp_ref[p, :, first : first + CHUNK] = weights
            prob_ref[:, first : first + CHUNK] = weights.astype(jnp.bfloat16)
            totals += jnp.sum(weights, axis=1, keepdims=True)
        mixed = dot_nn(prob_ref[...], kv_ref[p, :, width : 2 * width])
        inv_tot[p] = jnp.broadcast_to(1.0 / totals, (rows, 128))
        att_ref[p] = narrow(mixed / totals).astype(jnp.bfloat16)
        return carry

    lax.fori_loop(0, pat_dev, forward, 0)
    loads[2].wait()
    loads[3].wait()

    def flat(values):
        return values.reshape(values.shape[0] * lat_dev, width)

    x_own = dot_nn(flat(att_ref[...]), w_out_ref[...]).astype(jnp.bfloat16)
    x_ext[HALO : HALO + pat_dev] = x_own.reshape(pat_dev, lat_dev, width)
    start_pair(x_pair)
    arrive_pair(x_pair)
    arrive_pair(cot_pair)

    def inside(count, before):
        window = (
            lax.broadcasted_iota(jnp.int32, (count * lat_dev, width), 0) // lat_dev
            + tm * pat_dev
            - before
        )
        return jnp.logical_and(window >= 0, window < times * pat_dev)

    wide0 = pat_dev + 4
    pre0 = bias_ref[0:1, :]
    for j in range(KSIZE):
        pre0 = pre0 + dot_nn(flat(x_ext[j : j + wide0]), conv_ref[0, j])
    x1 = flat(x_ext[1 : 1 + wide0]).astype(jnp.float32) + pre0 * jax.nn.sigmoid(pre0)
    x1 = jnp.where(inside(wide0, 2), x1, 0.0).astype(jnp.bfloat16)
    pre1 = bias_ref[1:2, :]
    span = pat_dev * lat_dev
    for j in range(KSIZE):
        first = 2 * j * lat_dev
        pre1 = pre1 + dot_nn(x1[first : first + span], conv_ref[1, j])
    first = 2 * lat_dev
    x2 = x1[first : first + span].astype(jnp.float32) + pre1 * jax.nn.sigmoid(pre1)
    feat_ref[...] = x2.astype(jnp.bfloat16).reshape(pat_dev, lat_dev, width)

    cot_own = flat(cot_ref[...]).astype(jnp.float32)
    gpre1 = (cot_own * silu_slope(pre1)).astype(jnp.bfloat16)
    g_ext[HALO : HALO + pat_dev] = gpre1.reshape(pat_dev, lat_dev, width)
    start_pair(g_pair)
    arrive_pair(g_pair)

    wide1 = pat_dev + 2
    g1 = jnp.concatenate(
        [cot_halo[0].astype(jnp.float32), cot_own, cot_halo[1].astype(jnp.float32)], axis=0
    )
    for j in range(KSIZE):
        g1 = g1 + dot_nt(flat(g_ext[4 - 2 * j : 4 - 2 * j + wide1]), conv_ref[1, j])
    gpre0 = g1 * silu_slope(pre0[lat_dev : lat_dev + wide1 * lat_dev])
    gpre0 = jnp.where(inside(wide1, 1), gpre0, 0.0).astype(jnp.bfloat16)
    gpre_ref[...] = gpre0.reshape(wide1, lat_dev, width)
    g1_ref[...] = g1
    g0 = dot_nt(flat(gpre_ref[2 : 2 + pat_dev]), conv_ref[0, 0])
    for j in range(1, KSIZE):
        g0 = g0 + dot_nt(flat(gpre_ref[2 - j : 2 - j + pat_dev]), conv_ref[0, j])
    g0 = g0 + g1_ref[lat_dev : lat_dev + span]
    grad_att = dot_nt(g0.astype(jnp.bfloat16), w_out_ref[...]).astype(jnp.bfloat16)
    sent_pair(x_pair)
    x_ext[HALO : HALO + pat_dev] = grad_att.reshape(pat_dev, lat_dev, width)

    dq_acc[...] = jnp.zeros((rows, width), jnp.float32)

    def backward(p, carry):
        grad_wide = widen(x_ext[HALO + p].astype(jnp.float32))
        att_wide = jnp.concatenate([att_ref[p].astype(jnp.float32)] * heads, axis=0)
        delta = jnp.sum(grad_wide * att_wide, axis=1, keepdims=True)
        grad_wide = grad_wide.astype(jnp.bfloat16)
        scale = inv_tot[p][:, 0:1]
        for first in range(0, contacts, CHUNK):
            grad_prob = dot_nt(grad_wide, kv_ref[p, first : first + CHUNK, width : 2 * width])
            prob = exp_ref[p, :, first : first + CHUNK] * scale
            prob_ref[:, first : first + CHUNK] = (prob * (grad_prob - delta)).astype(jnp.bfloat16)
        dq_acc[...] += dot_nn(prob_ref[...], kv_ref[p, :, 0:width])
        return carry

    lax.fori_loop(0, pat_dev, backward, 0)

    dq_parts[tm] = narrow(dq_acc[...]) * scale_dot

    def part_copy(k):
        return remote(
            dq_parts.at[tm],
            dq_parts.at[tm],
            part_send.at[k],
            part_recv.at[k],
            me,
            lax.rem(tm + k, times),
        )

    own_rows = pl.ds(pl.multiple_of(me * lat_dev, lat_dev), lat_dev)

    def all_copy(k):
        return remote(
            dq_all.at[own_rows],
            dq_all.at[own_rows],
            all_send.at[k],
            all_recv.at[k],
            lax.rem(me + k, groups),
            tm,
        )

    for k in range(1, times):
        part_copy(k).start()
    for k in range(1, times):
        part_copy(k).wait_recv()
    dq_sum = dq_parts[0]
    for t in range(1, times):
        dq_sum = dq_sum + dq_parts[t]
    dq_all[own_rows, :] = dq_sum.astype(jnp.bfloat16)
    for k in range(1, groups):
        all_copy(k).start()
    for k in range(1, groups):
        all_copy(k).wait_recv()
    dlat_ref[...] = dot_nt(dq_all[...], w_query_ref[...])

    for k in range(1, groups):
        idx_copy(k).wait_send()
        sig_copy(k).wait_send()
        all_copy(k).wait_send()
    for pair in range(groups // 2):
        pos_copy(2 * pair + core).wait_send()
    for k in range(1, times):
        part_copy(k).wait_send()
    sent_pair(cot_pair)
    sent_pair(g_pair)


def fused(
    signal,
    pos_idx,
    live_count,
    latents,
    pos_table,
    w_in,
    w_kv,
    w_query,
    w_out,
    conv_weight,
    conv_bias,
    cotangent,
):
    con_dev, width_sig = signal.shape
    pat_dev = width_sig // PATCH
    groups, times = lax.axis_size("contacts"), lax.axis_size("tm")
    lat_rows, width = latents.shape
    lat_dev = lat_rows // groups
    rows = width // HD * lat_dev
    contacts = groups * con_dev
    is_valid = jnp.arange(con_dev, dtype=jnp.int32) < live_count[0]
    spots = jnp.broadcast_to(jnp.where(is_valid, pos_idx, -1)[None], (8, con_dev))
    bf16, f32 = jnp.bfloat16, jnp.float32
    vmem = pl.BlockSpec(memory_space=pltpu.VMEM)
    away = pl.BlockSpec(memory_space=pl.ANY)
    dma = pltpu.SemaphoreType.DMA
    return pl.pallas_call(
        functools.partial(fused_kernel, groups, times),
        out_shape=(
            jax.ShapeDtypeStruct((pat_dev, lat_dev, width), bf16),
            jax.ShapeDtypeStruct((lat_rows, width), f32),
        ),
        in_specs=[vmem] * 7 + [away] * 4,
        out_specs=(vmem, vmem),
        scratch_shapes=[
            pltpu.VMEM(pos_table.shape, bf16),
            pltpu.VMEM(w_kv.shape, bf16),
            pltpu.VMEM(w_out.shape, bf16),
            pltpu.VMEM(conv_weight.shape, bf16),
            pltpu.VMEM((groups, con_dev, width_sig), bf16),
            pltpu.VMEM((groups, 8, con_dev), jnp.int32),
            pltpu.VMEM((pat_dev, width_sig, width), bf16),
            pltpu.VMEM((groups, con_dev, width), bf16),
            pltpu.VMEM((8, contacts), f32),
            pltpu.VMEM((pat_dev, contacts, 2 * width), bf16),
            pltpu.VMEM((pat_dev, rows, contacts), f32),
            pltpu.VMEM((rows, contacts), bf16),
            pltpu.VMEM((pat_dev, rows, 128), f32),
            pltpu.VMEM((rows, width), bf16),
            pltpu.VMEM((pat_dev, lat_dev, width), bf16),
            pltpu.VMEM((2, lat_dev, width), bf16),
            pltpu.VMEM((pat_dev + 2 * HALO, lat_dev, width), bf16),
            pltpu.VMEM((pat_dev + 2 * HALO, lat_dev, width), bf16),
            pltpu.VMEM((pat_dev + 2, lat_dev, width), bf16),
            pltpu.VMEM(((pat_dev + 2) * lat_dev, width), f32),
            pltpu.VMEM((rows, width), f32),
            pltpu.VMEM((times, lat_dev, width), f32),
            pltpu.VMEM((lat_rows, width), bf16),
            dma((4,)),
            dma((groups,)),
            dma((groups,)),
            dma((groups,)),
            dma((groups,)),
            dma((groups,)),
            dma((groups,)),
            dma((6,)),
            dma((6,)),
            dma((times,)),
            dma((times,)),
            dma((groups,)),
            dma((groups,)),
        ],
        compiler_params=pltpu.CompilerParams(
            collective_id=0, has_side_effects=True, vmem_limit_bytes=VMEM_CAP
        ),
    )(
        signal,
        spots,
        latents,
        w_in,
        w_query,
        conv_bias,
        cotangent,
        pos_table,
        w_kv,
        w_out,
        conv_weight,
    )


def device_program(*args):
    signal, latents = args[0], args[3]
    groups = lax.axis_size("contacts")
    pat_dev = signal.shape[1] // PATCH
    lat_dev = latents.shape[0] // groups
    held = groups * signal.shape[0] * pat_dev * latents.shape[1] * 4
    paired = groups % 2 == 0 and lax.axis_size("tm") % 2 == 0
    if paired and lat_dev % 16 == 0 and pat_dev >= HALO and held <= 24 * 1024 * 1024:
        return fused(*args)
    return local(*args)


def solution(mesh):
    in_specs = (
        P("contacts", "tm"),
        P("contacts"),
        P("contacts"),
        P(),
        P(),
        P(),
        P(),
        P(),
        P(),
        P(),
        P(),
        P("tm", "contacts", None),
    )
    out_specs = (P("tm", "contacts", None), P())
    return jax.shard_map(
        device_program, mesh=mesh, in_specs=in_specs, out_specs=out_specs, check_vma=False
    )
```

```python
import functools

import jax
import jax.numpy as jnp
from jax import lax
from jax.experimental import pallas as pl
from jax.experimental.pallas import tpu as pltpu
from jax.sharding import PartitionSpec as P

HD = 64
PATCH = 32
KSIZE = 3
LAYERS = 2


neg_big = -1e30
scale_dot = 0.125


def with_halo(x, sides, width):
    for axis, dim in sides:
        peers, length = (lax.axis_size(axis), x.shape[dim])
        up = [(i, (i + 1) % peers) for i in range(peers - 1)]
        down = [(j, i) for i, j in up]
        last = lax.slice_in_dim(x, length - width, length, axis=dim)
        first = lax.slice_in_dim(x, 0, width, axis=dim)
        before = lax.ppermute(last, axis, up)
        after = lax.ppermute(first, axis, down)
        x = jnp.concatenate([before, x, after], axis=dim)
    return x


def silu_slope(pre_act):
    sigmoid_v = jax.nn.sigmoid(pre_act)
    return sigmoid_v * (1.0 + pre_act * (1.0 - sigmoid_v))


def split_heads(values, head_count):
    return values.reshape(values.shape[:-1] + (head_count, values.shape[-1] // head_count))


def normalize(accum_out, totals):
    head_count = totals.shape[-1]
    return (
        (split_heads(accum_out, head_count) / totals[..., None])
        .reshape(accum_out.shape)
        .astype(jnp.bfloat16)
    )


def conv_apply(source, weight, bias_row, dilation, out_count):
    stacked = jnp.stack(
        [source[j * dilation : j * dilation + out_count] for j in range(KSIZE)], axis=2
    )
    return (
        jnp.einsum("tlji,jio->tlo", stacked, weight, preferred_element_type=jnp.float32) + bias_row
    )


def local(
    signal,
    pos_idx,
    live_count,
    latents,
    pos_table,
    w_in,
    w_kv,
    w_query,
    w_out,
    conv_weight,
    conv_bias,
    cotangent,
):
    con_dev = signal.shape[0]
    pat_dev = signal.shape[1] // PATCH
    model_width = w_query.shape[0]
    head_count = model_width // HD
    lat_rows = latents.shape[0]
    groups = lax.axis_size("contacts")
    lat_dev = lat_rows // groups
    is_valid = jnp.arange(con_dev, dtype=jnp.int32) < live_count[0]
    embedded = jnp.einsum(
        "cpt,td->pcd",
        signal.reshape(con_dev, pat_dev, PATCH),
        w_in,
        preferred_element_type=jnp.float32,
    )
    pos_rows = jnp.take(pos_table, pos_idx, axis=0).astype(jnp.float32)
    tokens = (embedded + pos_rows[None]).astype(jnp.bfloat16)
    keyval = jnp.dot(
        tokens.reshape(pat_dev * con_dev, model_width), w_kv, preferred_element_type=jnp.float32
    ).astype(jnp.bfloat16)
    keyval = keyval.reshape(pat_dev // 2, 2, con_dev, 2, head_count, HD)
    queries = (
        jnp.dot(latents, w_query, preferred_element_type=jnp.float32)
        .astype(jnp.bfloat16)
        .reshape(lat_rows, head_count, HD)
    )

    def masked_scores(key_block):
        scores = (
            jnp.einsum("ihe,pche->phic", queries, key_block, preferred_element_type=jnp.float32)
            * scale_dot
        )
        return jnp.where(is_valid, scores, neg_big)

    def attend(kv_block):
        scores = masked_scores(kv_block[:, :, 0])
        top_score = jnp.max(scores, axis=3)
        weights = jnp.where(is_valid, jnp.exp(scores - top_score[..., None]), 0.0)
        totals = jnp.sum(weights, axis=3)
        accum_out = jnp.einsum(
            "phic,pche->pihe",
            weights.astype(jnp.bfloat16),
            kv_block[:, :, 1],
            preferred_element_type=jnp.float32,
        )
        return (
            jnp.swapaxes(top_score, 1, 2),
            jnp.swapaxes(totals, 1, 2),
            accum_out.reshape(2, lat_rows, model_width),
        )

    top_score, totals, accum_out = lax.map(attend, keyval)
    top_score = top_score.reshape(pat_dev, lat_rows, head_count)
    totals = totals.reshape(pat_dev, lat_rows, head_count)
    accum_out = accum_out.reshape(pat_dev, lat_rows, model_width)
    got_top, got_total, got_acc = (
        lax.all_to_all(top_score[None], "contacts", split_axis=2, concat_axis=0, tiled=True),
        lax.all_to_all(totals[None], "contacts", split_axis=2, concat_axis=0, tiled=True),
        lax.all_to_all(accum_out[None], "contacts", split_axis=2, concat_axis=0, tiled=True),
    )
    own_top = jnp.max(got_top, axis=0)
    factor = jnp.exp(got_top - own_top[None])
    own_total = jnp.sum(got_total * factor, axis=0)
    own_acc = jnp.sum(split_heads(got_acc, head_count) * factor[..., None], axis=0).reshape(
        pat_dev, lat_dev, model_width
    )
    attended = normalize(own_acc, own_total)
    start_x = (
        jnp.dot(
            attended.reshape(pat_dev * lat_dev, model_width),
            w_out,
            preferred_element_type=jnp.float32,
        )
        .astype(jnp.bfloat16)
        .reshape(pat_dev, lat_dev, model_width)
    )
    hidden_list = []
    current = start_x
    for layer_no in range(LAYERS):
        dilation = 2**layer_no
        padded = with_halo(current, (("tm", 0),), dilation * (KSIZE // 2))
        pre_act = conv_apply(padded, conv_weight[layer_no], conv_bias[layer_no], dilation, pat_dev)
        current = (current.astype(jnp.float32) + jax.nn.silu(pre_act)).astype(jnp.bfloat16)
        hidden_list.append(pre_act)
    grad_now = cotangent.astype(jnp.float32)
    for layer_no in reversed(range(LAYERS)):
        dilation = 2**layer_no
        grad_pre = (grad_now * silu_slope(hidden_list[layer_no])).astype(jnp.bfloat16)
        padded = with_halo(grad_pre, (("tm", 0),), dilation * (KSIZE // 2))
        stacked = jnp.stack(
            [
                padded[(KSIZE - 1 - j) * dilation : (KSIZE - 1 - j) * dilation + pat_dev]
                for j in range(KSIZE)
            ],
            axis=2,
        )
        grad_now = grad_now + jnp.einsum(
            "tljo,jio->tli", stacked, conv_weight[layer_no], preferred_element_type=jnp.float32
        )
    grad_att = lax.dot_general(
        grad_now.astype(jnp.bfloat16).reshape(pat_dev * lat_dev, model_width),
        w_out,
        (((1,), (1,)), ((), ())),
        preferred_element_type=jnp.float32,
    )
    grad_att = grad_att.astype(jnp.bfloat16).reshape(pat_dev, lat_dev, model_width)
    grad_all, attended_all = (
        lax.all_gather(grad_att, "contacts", axis=1, tiled=True),
        lax.all_gather(attended, "contacts", axis=1, tiled=True),
    )
    top_all, total_all = (
        lax.all_gather(own_top, "contacts", axis=1, tiled=True),
        lax.all_gather(own_total, "contacts", axis=1, tiled=True),
    )
    delta_row = jnp.sum(
        split_heads(grad_all.astype(jnp.float32), head_count)
        * split_heads(attended_all.astype(jnp.float32), head_count),
        axis=3,
    )

    def back_block(dq_sum, parts):
        kv_block, grad_block, top_block, total_block, delta_block = parts
        key_block = kv_block[:, :, 0]
        scores = masked_scores(key_block)
        top_now = jnp.swapaxes(top_block, 1, 2)
        total_now = jnp.swapaxes(total_block, 1, 2)
        prob_vals = jnp.where(
            is_valid, jnp.exp(scores - top_now[..., None]) / total_now[..., None], 0.0
        )
        grad_prob = jnp.einsum(
            "pihe,pche->phic",
            split_heads(grad_block, head_count),
            kv_block[:, :, 1],
            preferred_element_type=jnp.float32,
        )
        delta_now = jnp.swapaxes(delta_block, 1, 2)
        dscore = (prob_vals * (grad_prob - delta_now[..., None])).astype(jnp.bfloat16)
        return (
            dq_sum
            + jnp.einsum("phic,pche->ihe", dscore, key_block, preferred_element_type=jnp.float32),
            None,
        )

    pairs = pat_dev // 2
    dq_sum, unused = lax.scan(
        back_block,
        jnp.zeros((lat_rows, head_count, HD), jnp.float32),
        (
            keyval,
            grad_all.reshape(pairs, 2, lat_rows, model_width),
            top_all.reshape(pairs, 2, lat_rows, head_count),
            total_all.reshape(pairs, 2, lat_rows, head_count),
            delta_row.reshape(pairs, 2, lat_rows, head_count),
        ),
    )
    query_grad = lax.psum((dq_sum * scale_dot).reshape(lat_rows, model_width), ("contacts", "tm"))
    d_latents = lax.dot_general(
        query_grad.astype(jnp.bfloat16),
        w_query,
        (((1,), (1,)), ((), ())),
        preferred_element_type=jnp.float32,
    )
    return (current, d_latents)


MESH = pl.DeviceIdType.MESH
HALO = 3
CHUNK = 512
VMEM_CAP = 56 * 1024 * 1024


def dot_nn(lhs, rhs):
    return jnp.dot(lhs, rhs, preferred_element_type=jnp.float32)


def dot_nt(lhs, rhs):
    return lax.dot_general(lhs, rhs, (((1,), (1,)), ((), ())), preferred_element_type=jnp.float32)


def fused_kernel(
    groups,
    times,
    sig_ref,
    idx_ref,
    latents_ref,
    w_in_ref,
    w_query_ref,
    bias_ref,
    cot_ref,
    table_hbm,
    w_kv_hbm,
    w_out_hbm,
    conv_hbm,
    feat_ref,
    dlat_ref,
    table_ref,
    w_kv_ref,
    w_out_ref,
    conv_ref,
    sig_all,
    idx_all,
    w_wide,
    pos_rows,
    valid_ref,
    kv_ref,
    exp_ref,
    prob_ref,
    inv_tot,
    q_wide,
    att_ref,
    cot_halo,
    x_ext,
    g_ext,
    gpre_ref,
    g1_ref,
    dq_acc,
    dq_parts,
    dq_all,
    load_sem,
    idx_send,
    idx_recv,
    sig_send,
    sig_recv,
    pos_send,
    pos_recv,
    halo_send,
    halo_recv,
    part_send,
    part_recv,
    all_send,
    all_recv,
):
    me = lax.axis_index("contacts")
    tm = lax.axis_index("tm")
    con_dev, width_sig = sig_ref.shape
    pat_dev = width_sig // PATCH
    lat_dev, width = att_ref.shape[1:]
    heads = width // HD
    rows = heads * lat_dev
    contacts = groups * con_dev
    table_rows = table_ref.shape[0]

    loads = [
        pltpu.make_async_copy(src, dst, load_sem.at[n])
        for n, (src, dst) in enumerate(
            (
                (table_hbm, table_ref),
                (w_kv_hbm, w_kv_ref),
                (w_out_hbm, w_out_ref),
                (conv_hbm, conv_ref),
            )
        )
    ]
    for load in loads:
        load.start()

    barrier = pltpu.get_barrier_semaphore()
    for k in range(1, groups):
        pl.semaphore_signal(
            barrier, inc=1, device_id=(lax.rem(me + k, groups), tm), device_id_type=MESH
        )
    for k in range(1, times):
        pl.semaphore_signal(
            barrier, inc=1, device_id=(me, lax.rem(tm + k, times)), device_id_type=MESH
        )
    pl.semaphore_wait(barrier, groups + times - 2)

    def remote(src, dst, send, recv, contact_id, tm_id):
        return pltpu.make_async_remote_copy(
            src_ref=src,
            dst_ref=dst,
            send_sem=send,
            recv_sem=recv,
            device_id=(contact_id, tm_id),
            device_id_type=MESH,
        )

    def idx_copy(k):
        return remote(
            idx_ref, idx_all.at[me], idx_send.at[k], idx_recv.at[k], lax.rem(me + k, groups), tm
        )

    def sig_copy(k):
        return remote(
            sig_ref, sig_all.at[me], sig_send.at[k], sig_recv.at[k], lax.rem(me + k, groups), tm
        )

    def to_right(src, dst, n):
        return remote(src, dst, halo_send.at[n], halo_recv.at[n], me, tm + 1)

    def to_left(src, dst, n):
        return remote(src, dst, halo_send.at[n], halo_recv.at[n], me, tm - 1)

    has_left = tm > 0
    has_right = tm < times - 1

    cot_pair = (
        to_right(cot_ref.at[pl.ds(pat_dev - 1, 1)], cot_halo.at[pl.ds(0, 1)], 0),
        to_left(cot_ref.at[pl.ds(0, 1)], cot_halo.at[pl.ds(1, 1)], 1),
    )

    def ext_pair(ext, n):
        return (
            to_right(ext.at[pl.ds(pat_dev, HALO)], ext.at[pl.ds(0, HALO)], n),
            to_left(ext.at[pl.ds(HALO, HALO)], ext.at[pl.ds(HALO + pat_dev, HALO)], n + 1),
        )

    x_pair = ext_pair(x_ext, 2)
    g_pair = ext_pair(g_ext, 4)

    def start_pair(pair):
        @pl.when(has_right)
        def _():
            pair[0].start()

        @pl.when(has_left)
        def _():
            pair[1].start()

    def arrive_pair(pair):
        @pl.when(has_left)
        def _():
            pair[0].wait_recv()

        @pl.when(has_right)
        def _():
            pair[1].wait_recv()

    def sent_pair(pair):
        @pl.when(has_right)
        def _():
            pair[0].wait_send()

        @pl.when(has_left)
        def _():
            pair[1].wait_send()

    for k in range(1, groups):
        idx_copy(k).start()
    for k in range(1, groups):
        sig_copy(k).start()
    start_pair(cot_pair)

    @pl.when(jnp.logical_not(has_left))
    def _():
        x_ext[0:HALO] = jnp.zeros((HALO, lat_dev, width), jnp.bfloat16)
        g_ext[0:HALO] = jnp.zeros((HALO, lat_dev, width), jnp.bfloat16)
        cot_halo[0:1] = jnp.zeros((1, lat_dev, width), jnp.bfloat16)

    @pl.when(jnp.logical_not(has_right))
    def _():
        x_ext[HALO + pat_dev :] = jnp.zeros((HALO, lat_dev, width), jnp.bfloat16)
        g_ext[HALO + pat_dev :] = jnp.zeros((HALO, lat_dev, width), jnp.bfloat16)
        cot_halo[1:2] = jnp.zeros((1, lat_dev, width), jnp.bfloat16)

    idx_all[me] = idx_ref[...]
    sig_all[me] = sig_ref[...]

    for p in range(pat_dev):
        w_wide[p] = jnp.zeros((width_sig, width), jnp.bfloat16)
        w_wide[p, p * PATCH : (p + 1) * PATCH, :] = w_in_ref[...]

    own_head = (
        lax.broadcasted_iota(jnp.int32, (rows, width), 0) // lat_dev
        == lax.broadcasted_iota(jnp.int32, (rows, width), 1) // HD
    )

    def widen(values):
        return jnp.where(own_head, jnp.concatenate([values] * heads, axis=0), 0.0)

    def narrow(values):
        return jnp.sum(jnp.where(own_head, values, 0.0).reshape(heads, lat_dev, width), axis=0)

    own_latents = latents_ref[pl.ds(pl.multiple_of(me * lat_dev, lat_dev), lat_dev), :]
    queries = dot_nn(own_latents, w_query_ref[...]).astype(jnp.bfloat16).astype(jnp.float32)
    q_wide[...] = widen(queries * scale_dot).astype(jnp.bfloat16)

    loads[0].wait()

    core = lax.rem(tm, 2)
    sibling = tm + 1 - 2 * core

    def pos_copy(k):
        block = lax.rem(me - k + groups, groups)
        return remote(
            pos_rows.at[block], pos_rows.at[block], pos_send.at[k], pos_recv.at[k], me, sibling
        )

    def mark_valid(k):
        block = lax.rem(me - k + groups, groups)
        start = pl.multiple_of(block * con_dev, con_dev)
        valid_ref[:, pl.ds(start, con_dev)] = jnp.where(idx_all[block] >= 0, 1.0, 0.0)

    def gather_block(pair, carry):
        @pl.when(pair > 0)
        def _():
            idx_copy(2 * pair).wait_recv()

        idx_copy(2 * pair + 1).wait_recv()
        mark_valid(2 * pair)
        mark_valid(2 * pair + 1)
        k = 2 * pair + core
        block = lax.rem(me - k + groups, groups)
        idx_rows = idx_all[block]
        column = jnp.transpose(
            jnp.broadcast_to(idx_rows[0:1].astype(jnp.float32), (128, con_dev))
        ).astype(jnp.int32)[:, 0:1]
        total = jnp.zeros((con_dev, width), jnp.float32)
        for first in range(0, table_rows, CHUNK):
            spots = lax.broadcasted_iota(jnp.int32, (con_dev, CHUNK), 1) + first
            hot = jnp.where(column == spots, 1.0, 0.0).astype(jnp.bfloat16)
            total += dot_nn(hot, table_ref[first : first + CHUNK, :])
        pos_rows[block] = total.astype(jnp.bfloat16)
        pos_copy(k).start()
        return carry

    lax.fori_loop(0, groups // 2, gather_block, 0)
    loads[1].wait()

    def project_block(k, carry):
        @pl.when(k > 0)
        def _():
            sig_copy(k).wait_recv()

        @pl.when(lax.rem(k, 2) != core)
        def _():
            pos_copy(k).wait_recv()

        block = lax.rem(me - k + groups, groups)
        sig_block = sig_all[block]
        pos_block = pos_rows[block].astype(jnp.float32)
        start = pl.multiple_of(block * con_dev, con_dev)
        for p in range(pat_dev):
            tokens = (dot_nn(sig_block, w_wide[p]) + pos_block).astype(jnp.bfloat16)
            kv_ref[p, pl.ds(start, con_dev), :] = dot_nn(tokens, w_kv_ref[...]).astype(
                jnp.bfloat16
            )
        return carry

    lax.fori_loop(0, groups, project_block, 0)

    def forward(p, carry):
        top = jnp.full((rows, 1), neg_big, jnp.float32)
        for first in range(0, contacts, CHUNK):
            scores = dot_nt(q_wide[...], kv_ref[p, first : first + CHUNK, 0:width])
            scores = jnp.where(valid_ref[0:1, first : first + CHUNK] > 0.0, scores, neg_big)
            exp_ref[p, :, first : first + CHUNK] = scores
            top = jnp.maximum(top, jnp.max(scores, axis=1, keepdims=True))
        totals = jnp.zeros((rows, 1), jnp.float32)
        for first in range(0, contacts, CHUNK):
            weights = jnp.exp(exp_ref[p, :, first : first + CHUNK] - top)
            exp_ref[p, :, first : first + CHUNK] = weights
            prob_ref[p, :, first : first + CHUNK] = weights.astype(jnp.bfloat16)
            totals += jnp.sum(weights, axis=1, keepdims=True)
        mixed = dot_nn(prob_ref[p], kv_ref[p, :, width : 2 * width])
        inv_tot[p] = jnp.broadcast_to(1.0 / totals, (rows, 128))
        att_ref[p] = narrow(mixed / totals).astype(jnp.bfloat16)
        return carry

    for p in range(pat_dev):
        forward(p, 0)
    loads[2].wait()
    loads[3].wait()

    def flat(values):
        return values.reshape(values.shape[0] * lat_dev, width)

    x_own = dot_nn(flat(att_ref[...]), w_out_ref[...]).astype(jnp.bfloat16)
    x_ext[HALO : HALO + pat_dev] = x_own.reshape(pat_dev, lat_dev, width)
    start_pair(x_pair)
    arrive_pair(x_pair)
    arrive_pair(cot_pair)

    def inside(count, before):
        window = (
            lax.broadcasted_iota(jnp.int32, (count * lat_dev, width), 0) // lat_dev
            + tm * pat_dev
            - before
        )
        return jnp.logical_and(window >= 0, window < times * pat_dev)

    wide0 = pat_dev + 4
    pre0 = bias_ref[0:1, :]
    for j in range(KSIZE):
        pre0 = pre0 + dot_nn(flat(x_ext[j : j + wide0]), conv_ref[0, j])
    x1 = flat(x_ext[1 : 1 + wide0]).astype(jnp.float32) + pre0 * jax.nn.sigmoid(pre0)
    x1 = jnp.where(inside(wide0, 2), x1, 0.0).astype(jnp.bfloat16)
    pre1 = bias_ref[1:2, :]
    span = pat_dev * lat_dev
    for j in range(KSIZE):
        first = 2 * j * lat_dev
        pre1 = pre1 + dot_nn(x1[first : first + span], conv_ref[1, j])
    first = 2 * lat_dev
    x2 = x1[first : first + span].astype(jnp.float32) + pre1 * jax.nn.sigmoid(pre1)
    feat_ref[...] = x2.astype(jnp.bfloat16).reshape(pat_dev, lat_dev, width)

    cot_own = flat(cot_ref[...]).astype(jnp.float32)
    gpre1 = (cot_own * silu_slope(pre1)).astype(jnp.bfloat16)
    g_ext[HALO : HALO + pat_dev] = gpre1.reshape(pat_dev, lat_dev, width)
    start_pair(g_pair)
    arrive_pair(g_pair)

    wide1 = pat_dev + 2
    g1 = jnp.concatenate(
        [cot_halo[0].astype(jnp.float32), cot_own, cot_halo[1].astype(jnp.float32)], axis=0
    )
    for j in range(KSIZE):
        g1 = g1 + dot_nt(flat(g_ext[4 - 2 * j : 4 - 2 * j + wide1]), conv_ref[1, j])
    gpre0 = g1 * silu_slope(pre0[lat_dev : lat_dev + wide1 * lat_dev])
    gpre0 = jnp.where(inside(wide1, 1), gpre0, 0.0).astype(jnp.bfloat16)
    gpre_ref[...] = gpre0.reshape(wide1, lat_dev, width)
    g1_ref[...] = g1
    g0 = dot_nt(flat(gpre_ref[2 : 2 + pat_dev]), conv_ref[0, 0])
    for j in range(1, KSIZE):
        g0 = g0 + dot_nt(flat(gpre_ref[2 - j : 2 - j + pat_dev]), conv_ref[0, j])
    g0 = g0 + g1_ref[lat_dev : lat_dev + span]
    grad_att = dot_nt(g0.astype(jnp.bfloat16), w_out_ref[...]).astype(jnp.bfloat16)
    sent_pair(x_pair)
    x_ext[HALO : HALO + pat_dev] = grad_att.reshape(pat_dev, lat_dev, width)

    dq_acc[...] = jnp.zeros((rows, width), jnp.float32)

    def backward(p, carry):
        grad_wide = widen(x_ext[HALO + p].astype(jnp.float32))
        att_wide = jnp.concatenate([att_ref[p].astype(jnp.float32)] * heads, axis=0)
        delta = jnp.sum(grad_wide * att_wide, axis=1, keepdims=True)
        grad_wide = grad_wide.astype(jnp.bfloat16)
        scale = inv_tot[p][:, 0:1]
        for first in range(0, contacts, CHUNK):
            grad_prob = dot_nt(grad_wide, kv_ref[p, first : first + CHUNK, width : 2 * width])
            prob = exp_ref[p, :, first : first + CHUNK] * scale
            prob_ref[p, :, first : first + CHUNK] = (prob * (grad_prob - delta)).astype(jnp.bfloat16)
        dq_acc[...] += dot_nn(prob_ref[p], kv_ref[p, :, 0:width])
        return carry

    for p in range(pat_dev):
        backward(p, 0)

    dq_parts[tm] = narrow(dq_acc[...]) * scale_dot

    def part_copy(k):
        return remote(
            dq_parts.at[tm],
            dq_parts.at[tm],
            part_send.at[k],
            part_recv.at[k],
            me,
            lax.rem(tm + k, times),
        )

    own_rows = pl.ds(pl.multiple_of(me * lat_dev, lat_dev), lat_dev)

    def all_copy(k):
        return remote(
            dq_all.at[own_rows],
            dq_all.at[own_rows],
            all_send.at[k],
            all_recv.at[k],
            lax.rem(me + k, groups),
            tm,
        )

    for k in range(1, times):
        part_copy(k).start()
    for k in range(1, times):
        part_copy(k).wait_recv()
    dq_sum = dq_parts[0]
    for t in range(1, times):
        dq_sum = dq_sum + dq_parts[t]
    dq_all[own_rows, :] = dq_sum.astype(jnp.bfloat16)
    for k in range(1, groups):
        all_copy(k).start()
    for k in range(1, groups):
        all_copy(k).wait_recv()
    dlat_ref[...] = dot_nt(dq_all[...], w_query_ref[...])

    for k in range(1, groups):
        idx_copy(k).wait_send()
        sig_copy(k).wait_send()
        all_copy(k).wait_send()
    for pair in range(groups // 2):
        pos_copy(2 * pair + core).wait_send()
    for k in range(1, times):
        part_copy(k).wait_send()
    sent_pair(cot_pair)
    sent_pair(g_pair)


def fused(
    signal,
    pos_idx,
    live_count,
    latents,
    pos_table,
    w_in,
    w_kv,
    w_query,
    w_out,
    conv_weight,
    conv_bias,
    cotangent,
):
    con_dev, width_sig = signal.shape
    pat_dev = width_sig // PATCH
    groups, times = lax.axis_size("contacts"), lax.axis_size("tm")
    lat_rows, width = latents.shape
    lat_dev = lat_rows // groups
    rows = width // HD * lat_dev
    contacts = groups * con_dev
    is_valid = jnp.arange(con_dev, dtype=jnp.int32) < live_count[0]
    spots = jnp.broadcast_to(jnp.where(is_valid, pos_idx, -1)[None], (8, con_dev))
    bf16, f32 = jnp.bfloat16, jnp.float32
    vmem = pl.BlockSpec(memory_space=pltpu.VMEM)
    away = pl.BlockSpec(memory_space=pl.ANY)
    dma = pltpu.SemaphoreType.DMA
    return pl.pallas_call(
        functools.partial(fused_kernel, groups, times),
        out_shape=(
            jax.ShapeDtypeStruct((pat_dev, lat_dev, width), bf16),
            jax.ShapeDtypeStruct((lat_rows, width), f32),
        ),
        in_specs=[vmem] * 7 + [away] * 4,
        out_specs=(vmem, vmem),
        scratch_shapes=[
            pltpu.VMEM(pos_table.shape, bf16),
            pltpu.VMEM(w_kv.shape, bf16),
            pltpu.VMEM(w_out.shape, bf16),
            pltpu.VMEM(conv_weight.shape, bf16),
            pltpu.VMEM((groups, con_dev, width_sig), bf16),
            pltpu.VMEM((groups, 8, con_dev), jnp.int32),
            pltpu.VMEM((pat_dev, width_sig, width), bf16),
            pltpu.VMEM((groups, con_dev, width), bf16),
            pltpu.VMEM((8, contacts), f32),
            pltpu.VMEM((pat_dev, contacts, 2 * width), bf16),
            pltpu.VMEM((pat_dev, rows, contacts), f32),
            pltpu.VMEM((pat_dev, rows, contacts), bf16),
            pltpu.VMEM((pat_dev, rows, 128), f32),
            pltpu.VMEM((rows, width), bf16),
            pltpu.VMEM((pat_dev, lat_dev, width), bf16),
            pltpu.VMEM((2, lat_dev, width), bf16),
            pltpu.VMEM((pat_dev + 2 * HALO, lat_dev, width), bf16),
            pltpu.VMEM((pat_dev + 2 * HALO, lat_dev, width), bf16),
            pltpu.VMEM((pat_dev + 2, lat_dev, width), bf16),
            pltpu.VMEM(((pat_dev + 2) * lat_dev, width), f32),
            pltpu.VMEM((rows, width), f32),
            pltpu.VMEM((times, lat_dev, width), f32),
            pltpu.VMEM((lat_rows, width), bf16),
            dma((4,)),
            dma((groups,)),
            dma((groups,)),
            dma((groups,)),
            dma((groups,)),
            dma((groups,)),
            dma((groups,)),
            dma((6,)),
            dma((6,)),
            dma((times,)),
            dma((times,)),
            dma((groups,)),
            dma((groups,)),
        ],
        compiler_params=pltpu.CompilerParams(
            collective_id=0, has_side_effects=True, vmem_limit_bytes=VMEM_CAP
        ),
    )(
        signal,
        spots,
        latents,
        w_in,
        w_query,
        conv_bias,
        cotangent,
        pos_table,
        w_kv,
        w_out,
        conv_weight,
    )


def device_program(*args):
    signal, latents = args[0], args[3]
    groups = lax.axis_size("contacts")
    pat_dev = signal.shape[1] // PATCH
    lat_dev = latents.shape[0] // groups
    held = groups * signal.shape[0] * pat_dev * latents.shape[1] * 4
    paired = groups % 2 == 0 and lax.axis_size("tm") % 2 == 0
    if paired and lat_dev % 16 == 0 and pat_dev >= HALO and held <= 24 * 1024 * 1024:
        return fused(*args)
    return local(*args)


def solution(mesh):
    in_specs = (
        P("contacts", "tm"),
        P("contacts"),
        P("contacts"),
        P(),
        P(),
        P(),
        P(),
        P(),
        P(),
        P(),
        P(),
        P("tm", "contacts", None),
    )
    out_specs = (P("tm", "contacts", None), P())
    return jax.shard_map(
        device_program, mesh=mesh, in_specs=in_specs, out_specs=out_specs, check_vma=False
    )
```
